32 devices in a mesh: pipe: 2 (over core), seq: 4 (over z), fsdp: 4 (over y, x).
Axes of the slice: x: 2, y: 2, z: 4, core: 2. Of those that a mesh axis runs over, the one named last changes fastest.
Arguments:
- section_input: bfloat16 [8, 256, 768], P('fsdp', 'seq'), may hold values from -6 to 6
- timesteps: int32 [8], P('fsdp'), may hold values from 0 to 999
- labels: int32 [8], P('fsdp'), may hold values from 0 to 999
- time_table: bfloat16 [1000, 768], P(None, 'fsdp'), may hold values from -5 to 5
- label_table: bfloat16 [1000, 768], P(None, 'fsdp'), may hold values from -5 to 5
- w_ada: bfloat16 [2, 768, 4608], P('pipe', 'fsdp'), may hold values from -0.21875 to 0.21875
- b_ada: bfloat16 [2, 4608], P('pipe', 'fsdp'), may hold values from -3 to 3
- w_qkv: bfloat16 [2, 768, 2304], P('pipe', 'fsdp'), may hold values from -0.21875 to 0.21875
- b_qv: bfloat16 [2, 1536], P('pipe', 'fsdp'), may hold values from -2 to 2
- w_out: bfloat16 [2, 768, 768], P('pipe', 'fsdp'), may hold values from -0.875 to 0.875
- b_out: bfloat16 [2, 768], P('pipe', 'fsdp'), may hold values from -2 to 2
- w_up: bfloat16 [2, 768, 3072], P('pipe', 'fsdp'), may hold values from -0.21875 to 0.21875
- b_up: bfloat16 [2, 3072], P('pipe', 'fsdp'), may hold values from -2 to 2
- w_down: bfloat16 [2, 3072, 768], P('pipe', 'fsdp'), may hold values from -0.15625 to 0.15625
- b_down: bfloat16 [2, 768], P('pipe', 'fsdp'), may hold values from -2 to 2
- out_grad: bfloat16 [8, 256, 768], P('fsdp', 'seq'), may hold values from -6 to 6
Outputs:
- section_out: bfloat16 [2, 8, 256, 768], P('pipe', 'fsdp', 'seq')
- section_in_grad: bfloat16 [2, 8, 256, 768], P('pipe', 'fsdp', 'seq')
- grad_time_table: float32 [1000, 768], P(None, 'fsdp')
- grad_label_table: float32 [1000, 768], P(None, 'fsdp')
- grad_w_ada: float32 [2, 768, 4608], P('pipe', 'fsdp')
- grad_b_ada: float32 [2, 4608], P('pipe', 'fsdp')
- grad_w_qkv: float32 [2, 768, 2304], P('pipe', 'fsdp')
- grad_b_qv: float32 [2, 1536], P('pipe', 'fsdp')
- grad_w_out: float32 [2, 768, 768], P('pipe', 'fsdp')
- grad_b_out: float32 [2, 768], P('pipe', 'fsdp')
- grad_w_up: float32 [2, 768, 3072], P('pipe', 'fsdp')
- grad_b_up: float32 [2, 3072], P('pipe', 'fsdp')
- grad_w_down: float32 [2, 3072, 768], P('pipe', 'fsdp')
- grad_b_down: float32 [2, 768], P('pipe', 'fsdp')
The draws below stay inside these ranges and needn't reach their ends.
All inputs are finite; a program needn't handle non-finite values.
Results may differ from the reference program's by a relative error of at most 0.02.
The reference program's roundings to bfloat16 on the way count: a program that leaves them out, or rounds other values in their place, can miss the bound.
Values may be sent and summed in bfloat16 or wider, within the bound.
A program may use at most 192 MiB of HBM per device.

```python
import math
import jax
import jax.numpy as jnp
from jax import lax

D = 768
FF = 3072
HEADS = 12
SEQ = 256
TIMES = 1000
CLASSES = 1000
HEAD_DIM = 64
LATENTS = 8


def touch_ends(entries, key, smallest, top_value):
    longest = entries.shape.index(max(entries.shape))
    spots = []
    for shift in (0, 1):
        where = [jax.random.randint(jax.random.fold_in(key, axis), (), 0, length) for axis, length in enumerate(entries.shape)]
        where[longest] = (where[longest] + shift) % entries.shape[longest]
        spots.append(tuple(where))
    return entries.at[spots[0]].set(smallest).at[spots[1]].set(top_value)


def raised(values, own_key, source, target, shards_of, factor):
    def block_of(axis_at):
        return (jnp.arange(values.shape[axis_at]) // (values.shape[axis_at] // shards_of)).reshape((-1,) + (1,) * (values.ndim - 1 - axis_at))

    near = jax.random.permutation(own_key, shards_of)[block_of(target)]
    other_side = (block_of(target) + shards_of // 2) % shards_of
    return jnp.where((block_of(source) == near) | (block_of(source) == other_side), factor * values, values)


def block_scale(stream_key, shape, shards, low, largest):
    gain = 1.0
    for dim, parts in shards:
        steps = jax.random.uniform(jax.random.fold_in(jax.random.fold_in(stream_key, 6), dim), (parts,), jnp.float32, low / len(shards), largest / len(shards))
        gain = gain * jnp.repeat(jnp.exp(steps), shape[dim] // parts).reshape((-1,) + (1,) * (len(shape) - 1 - dim))
    return gain


def centred(own_key, dims, scale, limit, cuts=(), kind=jnp.bfloat16):
    loudness = block_scale(own_key, dims, cuts, -0.22, 0.18) if cuts else 1.0
    entries = jax.random.normal(own_key, dims, jnp.float32) * scale * loudness
    return jnp.minimum(jnp.maximum(entries, -limit), limit).astype(kind)


def bell_draw_with(stream_key, shape, scale, most, cuts, heavy, held_as=jnp.bfloat16):
    drawn = scale * jax.random.normal(stream_key, shape, jnp.float32)
    if cuts:
        drawn = drawn * block_scale(stream_key, shape, cuts, -0.22, 0.18)
    return jnp.clip(raised(drawn, jax.random.fold_in(stream_key, 3), *heavy), -most, most).astype(held_as)


def setup_inputs(seed: int = 0) -> dict:
    splits = jax.random.split(jax.random.key(seed), 17)
    section_input = bell_draw_with(splits[0], (LATENTS, SEQ, D), 1.0, 6.0, ((0, 4), (1, 4)), (0, 2, 4, 2.0))
    timesteps = touch_ends(jax.random.randint(splits[1], (LATENTS,), 0, TIMES), jax.random.fold_in(splits[1], 1), 0, TIMES - 1).astype(jnp.int32)
    labels = touch_ends(jax.random.randint(splits[2], (LATENTS,), 0, CLASSES), jax.random.fold_in(splits[2], 1), 0, CLASSES - 1).astype(jnp.int32)
    time_table = centred(splits[3], (TIMES, D), 0.8, 5.0, ((1, 4),))
    label_table = centred(splits[4], (CLASSES, D), 0.8, 5.0, ((1, 4),))
    w_ada = centred(splits[5], (2, D, 6 * D), D ** -0.5, 0.21875, ((0, 2), (1, 4)))
    b_ada = centred(splits[6], (2, 6 * D), 0.5, 3.0, ((0, 2), (1, 4)))
    w_qkv = centred(splits[7], (2, D, 3 * D), D ** -0.5, 0.21875, ((0, 2), (1, 4)))
    b_qv = centred(splits[8], (2, 2 * D), 0.3, 2.0, ((0, 2), (1, 4)))
    w_out = centred(splits[9], (2, D, D), (D // 16) ** -0.5, 0.875, ((0, 2), (1, 4)))
    b_out = centred(splits[10], (2, D), 0.3, 2.0, ((0, 2), (1, 4)))
    w_up = centred(splits[11], (2, D, FF), D ** -0.5, 0.21875, ((0, 2), (1, 4)))
    b_up = centred(splits[12], (2, FF), 0.3, 2.0, ((0, 2), (1, 4)))
    w_down = centred(splits[13], (2, FF, D), (FF // 2) ** -0.5, 0.15625, ((0, 2), (1, 4)))
    b_down = centred(splits[14], (2, D), 0.3, 2.0, ((0, 2), (1, 4)))
    out_grad = bell_draw_with(splits[15], (LATENTS, SEQ, D), 1.0, 6.0, ((0, 4), (1, 4)), (0, 2, 4, 2.0))
    return {"section_input": section_input, "timesteps": timesteps, "labels": labels, "time_table": time_table, "label_table": label_table, "w_ada": w_ada, "b_ada": b_ada, "w_qkv": w_qkv, "b_qv": b_qv, "w_out": w_out, "b_out": b_out, "w_up": w_up, "b_up": b_up, "w_down": w_down, "b_down": b_down, "out_grad": out_grad}


@jax.custom_vjp
def low(v):
    return lax.optimization_barrier(v.astype(jnp.bfloat16)).astype(jnp.float32)

@jax.custom_vjp
def low_back(v):
    return v

def low_keep(v):
    return (low(v), None)

def low_pass(kept, grad):
    return (grad,)

def back_keep(v):
    return (v, None)

def back_low(kept, grad):
    return (low(grad),)
low.defvjp(low_keep, low_pass)
low_back.defvjp(back_keep, back_low)

def dense(rows, weight):
    return jnp.dot(rows, weight, precision=lax.Precision.HIGHEST)

def layer_norm(field):
    center = field - lax.optimization_barrier(jnp.mean(field, axis=-1, keepdims=True))
    spread = lax.optimization_barrier(jnp.mean(center * center, axis=-1, keepdims=True))
    return center * lax.rsqrt(spread + 1e-06)

def smooth_gate(value):
    return jax.nn.gelu(value, approximate=True)

def block(field, cond, weights):
    w_ada, b_ada, w_qkv, b_qv, w_out, b_out, w_up, b_up, w_down, b_down = weights
    group = field.shape[0]
    scaled = low(jax.nn.silu(cond))
    modulation = low_back(dense(scaled, w_ada) + b_ada)
    shift_one, scale_one, gate_one, shift_two, scale_two, gate_two = jnp.split(modulation, 6, axis=-1)
    first_in = low(layer_norm(field) * (1.0 + scale_one[:, None]) + shift_one[:, None])
    bias = jnp.concatenate([b_qv[:D], jnp.zeros((D,), jnp.float32), b_qv[D:]])
    joined = low(low_back(dense(first_in, w_qkv) + bias))
    joined = joined.reshape(group, SEQ, 3, HEADS, HEAD_DIM)
    queries = joined[:, :, 0]
    key_rows = joined[:, :, 1]
    values = joined[:, :, 2]
    scores = low_back(jnp.einsum('bqhd,bkhd->bhqk', queries, key_rows, precision=lax.Precision.HIGHEST) * HEAD_DIM ** (-0.5))
    probs = jax.nn.softmax(scores, axis=-1)
    attended = jnp.einsum('bhqk,bkhd->bqhd', low(probs), values, precision=lax.Precision.HIGHEST)
    attended = low(low_back(attended)).reshape(group, SEQ, D)
    branch = low_back(dense(attended, w_out) + b_out)
    middle = field + gate_one[:, None] * branch
    second_in = low(layer_norm(middle) * (1.0 + scale_two[:, None]) + shift_two[:, None])
    hidden = low_back(dense(second_in, w_up) + b_up)
    active = low(smooth_gate(hidden))
    result = low_back(dense(active, w_down) + b_down)
    return middle + gate_two[:, None] * result

def reference(section_input, timesteps, labels, time_table, label_table, w_ada, b_ada, w_qkv, b_qv, w_out, b_out, w_up, b_up, w_down, b_down, out_grad):
    weights = tuple((item.astype(jnp.float32) for item in (w_ada, b_ada, w_qkv, b_qv, w_out, b_out, w_up, b_up, w_down, b_down)))
    tables = (time_table.astype(jnp.float32), label_table.astype(jnp.float32))
    field = section_input.astype(jnp.float32)
    nudge = jnp.zeros_like(field)
    group = math.gcd(LATENTS, max(1, 4096 // SEQ))
    count = LATENTS // group

    def forward(field, nudge, tables, weights):
        cond = jnp.take(tables[0], timesteps, axis=0) + jnp.take(tables[1], labels, axis=0)
        first_params = tuple((item[0] for item in weights))
        second_params = tuple((item[1] for item in weights))

        def one_group(carry, item):
            rows, pushes, conds = item
            first = block(rows, conds, first_params)
            handed = low(low_back(first)) + pushes
            second = block(handed, conds, second_params)
            return (carry, (second, first))
        _, (seconds, firsts) = lax.scan(jax.checkpoint(one_group), jnp.zeros((), jnp.float32), (field.reshape(count, group, SEQ, D), nudge.reshape(count, group, SEQ, D), cond.reshape(count, group, D)))
        return (seconds.reshape(LATENTS, SEQ, D), firsts.reshape(LATENTS, SEQ, D))
    final, pullback, firsts = jax.vjp(forward, field, nudge, tables, weights, has_aux=True)
    d_field, d_nudge, d_tables, d_weights = pullback(out_grad.astype(jnp.float32))
    section_out = jnp.stack([firsts, final]).astype(jnp.bfloat16)
    section_in_grad = jnp.stack([d_field, d_nudge]).astype(jnp.bfloat16)
    return (section_out, section_in_grad, d_tables[0], d_tables[1], d_weights[0], d_weights[1], d_weights[2], d_weights[3], d_weights[4], d_weights[5], d_weights[6], d_weights[7], d_weights[8], d_weights[9])
```

```python
import jax
import jax.numpy as jnp
from jax import lax
from jax.sharding import PartitionSpec as P

HEADS = 12


def passed_along(x, axis, by):
    count = lax.axis_size(axis)
    pairs = [(i, i + by) for i in range(count) if 0 <= i + by < count]
    return lax.ppermute(x, axis, pairs)


def matmul(left, right):
    return lax.dot_general(
        left, right, (((left.ndim - 1,), (0,)), ((), ())), preferred_element_type=jnp.float32
    )


def against(left, right):
    return lax.dot_general(
        left, right, (((left.ndim - 1,), (1,)), ((), ())), preferred_element_type=jnp.float32
    )


def inner_rows(left, right):
    return lax.dot_general(
        left, right, (((0,), (0,)), ((), ())), preferred_element_type=jnp.float32
    )


def norm_parts(field):
    center = field - jnp.mean(field, axis=-1, keepdims=True)
    inverse = lax.rsqrt(jnp.mean(center * center, axis=-1, keepdims=True) + 1e-06)
    return (center * inverse, inverse)


def norm_back(normed, inverse, upstream):
    return inverse * (
        upstream
        - jnp.mean(upstream, axis=-1, keepdims=True)
        - normed * jnp.mean(upstream * normed, axis=-1, keepdims=True)
    )


def smooth_gate(value):
    return jax.nn.gelu(value, approximate=True)


def dots(pattern, left, right):
    return jnp.einsum(pattern, left, right, preferred_element_type=jnp.float32)


def by_head(rows, count):
    lats, length, width = rows.shape
    return rows.reshape(lats, length, count, width // count)


def attend_forward(queries, key_rows, values, factor):
    scores = dots("bqhd,bkhd->bhqk", queries, key_rows) * factor
    summit = jnp.max(scores, axis=-1, keepdims=True)
    raised = jnp.exp(scores - summit)
    probs = raised / jnp.sum(raised, axis=-1, keepdims=True)
    attended = dots("bhqk,bkhd->bqhd", probs.astype(jnp.bfloat16), values)
    return (attended.astype(jnp.bfloat16), probs)


def attend_backward(queries, key_rows, values, probs, d_attended, factor):
    d_probs = dots("bqhd,bkhd->bhqk", d_attended, values)
    delta = jnp.sum(probs * d_probs, axis=-1, keepdims=True)
    d_scores = (probs * (d_probs - delta)).astype(jnp.bfloat16)
    d_queries = dots("bhqk,bkhd->bqhd", d_scores, key_rows) * factor
    d_keys = dots("bhqk,bqhd->bkhd", d_scores, queries) * factor
    d_values = dots("bhqk,bqhd->bkhd", probs.astype(jnp.bfloat16), d_attended)
    return tuple(part.astype(jnp.bfloat16) for part in (d_queries, d_keys, d_values))


def local(
    section_input,
    timesteps,
    labels,
    time_table,
    label_table,
    w_ada,
    b_ada,
    w_qkv,
    b_qv,
    w_out,
    b_out,
    w_up,
    b_up,
    w_down,
    b_down,
    out_grad,
):
    section = lax.axis_index("pipe")
    shard = lax.axis_index("fsdp")
    shards = lax.axis_size("fsdp")
    groups = lax.axis_size("seq")
    lats, seq_dev, width = section_input.shape
    rows = lats * seq_dev
    full_seq = seq_dev * groups
    heads = HEADS // groups
    head_size = width // HEADS
    band = heads * head_size
    factor = head_size ** (-0.5)
    depth = w_qkv.shape[1]
    hidden_width = w_up.shape[2]

    ids = lax.all_gather(jnp.stack([timesteps, labels]), "fsdp", axis=1, tiled=True)
    bias_sizes = [item.shape[1] for item in (b_ada, b_qv, b_out, b_up, b_down)]
    biases = lax.all_gather(
        jnp.concatenate([b_ada[0], b_qv[0], b_out[0], b_up[0], b_down[0]]), "fsdp", axis=0
    )
    bias_full = []
    start = 0
    for size in bias_sizes:
        bias_full.append(biases[:, start : start + size].reshape(-1).astype(jnp.float32))
        start += size
    ada_bias, joined_bias, out_bias, up_bias, down_bias = bias_full

    by_group = w_qkv[0].reshape(depth, 3, groups, band).transpose(2, 0, 1, 3)
    joined_weight = lax.all_gather(
        by_group.reshape(groups, depth, 3 * band), "fsdp", axis=1, tiled=True
    )
    out_weight = lax.all_gather(w_out[0], "fsdp", axis=0, tiled=True).reshape(groups, band, width)
    up_weight = lax.all_gather(w_up[0], "fsdp", axis=0, tiled=True)
    down_weight = lax.all_gather(w_down[0], "fsdp", axis=0, tiled=True)
    bias_qkv = jnp.stack(
        [joined_bias[:width], jnp.zeros((width,), jnp.float32), joined_bias[width:]]
    )
    bias_qkv = bias_qkv.reshape(3, groups, band).transpose(1, 0, 2).reshape(groups, 1, 3 * band)

    time_hot = (ids[0][:, None] == jnp.arange(time_table.shape[0])[None, :]).astype(jnp.bfloat16)
    label_hot = (ids[1][:, None] == jnp.arange(label_table.shape[0])[None, :]).astype(jnp.bfloat16)
    cond = matmul(time_hot, time_table) + matmul(label_hot, label_table)
    scaled = jax.nn.silu(cond).astype(jnp.bfloat16)
    ada_terms = matmul(scaled, w_ada[0]).reshape(shards, lats, 6 * width)
    modulation = jnp.sum(lax.all_to_all(ada_terms, "fsdp", 0, 0), axis=0) + ada_bias
    shift1, scale1, gate1, shift2, scale2, gate2 = (
        part[:, None] for part in jnp.split(modulation, 6, axis=-1)
    )

    def to_heads(item):
        traded = lax.all_to_all(item, "seq", 0, 0)
        span = traded.shape[-1]
        traded = traded.reshape(groups, lats, seq_dev, span).transpose(1, 0, 2, 3)
        return traded.reshape(lats, full_seq, span)

    def to_tokens(item):
        span = item.shape[-1]
        item = item.reshape(lats, groups, seq_dev, span).transpose(1, 0, 2, 3)
        return lax.all_to_all(item.reshape(groups, rows, span), "seq", 0, 0)

    def flat(item):
        return item.reshape(rows, item.shape[-1])

    def tall(item):
        return item.reshape(lats, seq_dev, item.shape[-1])

    def section_forward(field):
        normed, inverse = norm_parts(field)
        first_in = (normed * (1.0 + scale1) + shift1).astype(jnp.bfloat16)
        joined = (dots("rd,pde->pre", flat(first_in), joined_weight) + bias_qkv).astype(
            jnp.bfloat16
        )
        joined = to_heads(joined)
        parts = tuple(by_head(part, heads) for part in jnp.split(joined, 3, axis=-1))
        attended, probs = attend_forward(*parts, factor)
        back = to_tokens(attended.reshape(lats, full_seq, band))
        branch = tall(dots("pre,pef->rf", back, out_weight) + out_bias)
        middle = field + gate1 * branch
        normed_mid, inverse_mid = norm_parts(middle)
        second_in = (normed_mid * (1.0 + scale2) + shift2).astype(jnp.bfloat16)
        hidden = matmul(flat(second_in), up_weight) + up_bias
        active = smooth_gate(hidden).astype(jnp.bfloat16)
        result = tall(matmul(active, down_weight) + down_bias)
        output = (middle + gate2 * result).astype(jnp.bfloat16)
        kept = (
            (normed, inverse, first_in),
            parts + (probs,),
            back,
            branch,
            (normed_mid, inverse_mid, second_in),
            hidden,
            active,
            result,
        )
        return (output, kept)

    def section_backward(upstream, kept):
        first, attention, back, branch, second, hidden, active, result = kept
        normed, inverse, first_in = first
        normed_mid, inverse_mid, second_in = second
        d_result = (gate2 * upstream).astype(jnp.bfloat16)
        d_active = against(flat(d_result), down_weight)
        _, gate_pull = jax.vjp(smooth_gate, hidden)
        d_hidden = gate_pull(d_active)[0].astype(jnp.bfloat16)
        d_second = tall(against(d_hidden, up_weight))
        d_middle = upstream + norm_back(normed_mid, inverse_mid, d_second * (1.0 + scale2))
        d_branch = (gate1 * d_middle).astype(jnp.bfloat16)
        d_back = dots("rf,pef->pre", flat(d_branch), out_weight).astype(jnp.bfloat16)
        d_parts = attend_backward(*attention, by_head(to_heads(d_back), heads), factor)
        d_joined = to_tokens(
            jnp.concatenate([part.reshape(lats, full_seq, band) for part in d_parts], axis=-1)
        )
        d_first = tall(dots("pre,pde->rd", d_joined, joined_weight))
        d_field = d_middle + norm_back(normed, inverse, d_first * (1.0 + scale1))
        d_field = d_field.astype(jnp.bfloat16)
        sums = (d_first, d_first * normed, d_middle * branch, d_second, d_second * normed_mid)
        d_mods = jnp.concatenate(
            [jnp.sum(item, axis=1) for item in sums + (upstream * result,)], axis=-1
        )
        return (d_field, d_mods, (d_joined, d_branch, d_hidden, d_result))

    handed, _ = section_forward(section_input.astype(jnp.float32))
    handed = passed_along(handed, "pipe", 1)
    entering = jnp.where(section == 0, section_input, handed)
    section_out, kept = section_forward(entering.astype(jnp.float32))
    handed, _, _ = section_backward(out_grad.astype(jnp.float32), kept)
    handed = passed_along(handed, "pipe", -1)
    upstream = jnp.where(section == 1, out_grad, handed).astype(jnp.float32)
    section_in_grad, d_mods, d_parts = section_backward(upstream, kept)
    d_joined, d_branch, d_hidden, d_result = d_parts
    d_branch, d_result = flat(d_branch), flat(d_result)

    def over_shards(part, dim):
        return lax.psum_scatter(
            part.astype(jnp.bfloat16), "fsdp", scatter_dimension=dim, tiled=True
        )

    in_order = d_joined.reshape(groups, rows, 3, band).transpose(1, 2, 0, 3)
    in_order = in_order.reshape(rows, 3 * width)
    grad_down = over_shards(inner_rows(kept[6], d_result), 0)
    grad_up = over_shards(inner_rows(flat(kept[4][2]), d_hidden), 0)
    grad_joined = over_shards(inner_rows(flat(kept[0][2]), in_order), 0)
    grad_out = over_shards(dots("pre,rf->pef", kept[2], d_branch).reshape(width, width), 0)
    def over_tokens(part):
        cut_up = part.reshape((groups, part.shape[0] // groups) + part.shape[1:])
        terms = lax.all_to_all(cut_up, "seq", 0, 0).astype(jnp.float32)
        own = jnp.sum(terms, axis=0).astype(jnp.bfloat16)
        whole = lax.all_to_all(jnp.broadcast_to(own[None], cut_up.shape), "seq", 0, 0)
        return whole.reshape(part.shape).astype(jnp.float32)

    grad_down = over_tokens(grad_down)
    grad_up = over_tokens(grad_up)
    grad_joined = over_tokens(grad_joined)
    grad_out = over_tokens(grad_out)

    placed = lax.dynamic_update_slice(
        jnp.zeros((shards * lats, 6 * width), jnp.float32), d_mods, (shard * lats, 0)
    )
    joined_sums = jnp.sum(d_joined, axis=1, dtype=jnp.float32).reshape(groups, 3, band)
    qv_sums = jnp.stack([joined_sums[:, 0], joined_sums[:, 2]])
    column_sums = [
        qv_sums.reshape(-1),
        jnp.sum(d_branch, axis=0, dtype=jnp.float32),
        jnp.sum(d_hidden, axis=0, dtype=jnp.float32),
        jnp.sum(d_result, axis=0, dtype=jnp.float32),
    ]
    small = lax.psum(jnp.concatenate([placed.reshape(-1)] + column_sums), ("fsdp", "seq"))
    cut = placed.size
    d_modulation = small[:cut].reshape(placed.shape).astype(jnp.bfloat16)

    def own_part(whole):
        size = whole.shape[0] // shards
        return lax.dynamic_slice_in_dim(whole, shard * size, size, 0)[None]

    bias_grads = []
    for part in column_sums:
        bias_grads.append(own_part(small[cut : cut + part.size]))
        cut += part.size
    grad_ada = inner_rows(scaled, d_modulation)
    grad_ada_bias = own_part(jnp.sum(d_modulation, axis=0, dtype=jnp.float32))
    d_scaled = against(d_modulation, w_ada[0])
    other = lax.ppermute(d_scaled, "pipe", [(0, 1), (1, 0)])
    _, silu_pull = jax.vjp(jax.nn.silu, cond)
    d_cond = silu_pull(d_scaled + other)[0]

    def table_grad(hot):
        return lax.dot_general(
            hot.astype(jnp.float32),
            d_cond,
            (((0,), (0,)), ((), ())),
            precision=lax.Precision.HIGHEST,
        )

    return (
        section_out[None],
        section_in_grad[None],
        table_grad(time_hot),
        table_grad(label_hot),
        grad_ada[None],
        grad_ada_bias,
        grad_joined[None],
        bias_grads[0],
        grad_out[None],
        bias_grads[1],
        grad_up[None],
        bias_grads[2],
        grad_down[None],
        bias_grads[3],
    )


def solution(mesh):
    in_specs = (
        P("fsdp", "seq", None),
        P("fsdp"),
        P("fsdp"),
        P(None, "fsdp"),
        P(None, "fsdp"),
        P("pipe", "fsdp", None),
        P("pipe", "fsdp"),
        P("pipe", "fsdp", None),
        P("pipe", "fsdp"),
        P("pipe", "fsdp", None),
        P("pipe", "fsdp"),
        P("pipe", "fsdp", None),
        P("pipe", "fsdp"),
        P("pipe", "fsdp", None),
        P("pipe", "fsdp"),
        P("fsdp", "seq", None),
    )
    out_specs = (
        P("pipe", "fsdp", "seq", None),
        P("pipe", "fsdp", "seq", None),
        P(None, "fsdp"),
        P(None, "fsdp"),
        P("pipe", "fsdp", None),
        P("pipe", "fsdp"),
        P("pipe", "fsdp", None),
        P("pipe", "fsdp"),
        P("pipe", "fsdp", None),
        P("pipe", "fsdp"),
        P("pipe", "fsdp", None),
        P("pipe", "fsdp"),
        P("pipe", "fsdp", None),
        P("pipe", "fsdp"),
    )
    return jax.shard_map(local, mesh=mesh, in_specs=in_specs, out_specs=out_specs, check_vma=False)
```

```python
import jax
import jax.numpy as jnp
from jax import lax
from jax.sharding import PartitionSpec as P

HEADS = 12


def passed_along(x, axis, by):
    count = lax.axis_size(axis)
    pairs = [(i, i + by) for i in range(count) if 0 <= i + by < count]
    return lax.ppermute(x, axis, pairs)


def matmul(left, right):
    return lax.dot_general(
        left, right, (((left.ndim - 1,), (0,)), ((), ())), preferred_element_type=jnp.float32
    )


def against(left, right):
    return lax.dot_general(
        left, right, (((left.ndim - 1,), (1,)), ((), ())), preferred_element_type=jnp.float32
    )


def inner_rows(left, right):
    return lax.dot_general(
        left, right, (((0,), (0,)), ((), ())), preferred_element_type=jnp.float32
    )


def norm_parts(field):
    center = field - jnp.mean(field, axis=-1, keepdims=True)
    inverse = lax.rsqrt(jnp.mean(center * center, axis=-1, keepdims=True) + 1e-06)
    return (center * inverse, inverse)


def norm_back(normed, inverse, upstream):
    return inverse * (
        upstream
        - jnp.mean(upstream, axis=-1, keepdims=True)
        - normed * jnp.mean(upstream * normed, axis=-1, keepdims=True)
    )


def smooth_gate(value):
    return jax.nn.gelu(value, approximate=True)


def dots(pattern, left, right):
    return jnp.einsum(pattern, left, right, preferred_element_type=jnp.float32)


def by_head(rows, count):
    lats, length, width = rows.shape
    return rows.reshape(lats, length, count, width // count)


def attend_forward(queries, key_rows, values, factor):
    scores = dots("bqhd,bkhd->bhqk", queries, key_rows) * factor
    summit = jnp.max(scores, axis=-1, keepdims=True)
    raised = jnp.exp(scores - summit)
    probs = raised / jnp.sum(raised, axis=-1, keepdims=True)
    attended = dots("bhqk,bkhd->bqhd", probs.astype(jnp.bfloat16), values)
    return (attended.astype(jnp.bfloat16), probs)


def attend_backward(queries, key_rows, values, probs, d_attended, factor):
    d_probs = dots("bqhd,bkhd->bhqk", d_attended, values)
    delta = jnp.sum(probs * d_probs, axis=-1, keepdims=True)
    d_scores = (probs * (d_probs - delta)).astype(jnp.bfloat16)
    d_queries = dots("bhqk,bkhd->bqhd", d_scores, key_rows) * factor
    d_keys = dots("bhqk,bqhd->bkhd", d_scores, queries) * factor
    d_values = dots("bhqk,bqhd->bkhd", probs.astype(jnp.bfloat16), d_attended)
    return tuple(part.astype(jnp.bfloat16) for part in (d_queries, d_keys, d_values))


def local(
    section_input,
    timesteps,
    labels,
    time_table,
    label_table,
    w_ada,
    b_ada,
    w_qkv,
    b_qv,
    w_out,
    b_out,
    w_up,
    b_up,
    w_down,
    b_down,
    out_grad,
):
    section = lax.axis_index("pipe")
    shard = lax.axis_index("fsdp")
    shards = lax.axis_size("fsdp")
    groups = lax.axis_size("seq")
    lats, seq_dev, width = section_input.shape
    rows = lats * seq_dev
    full_seq = seq_dev * groups
    heads = HEADS // groups
    head_size = width // HEADS
    band = heads * head_size
    factor = head_size ** (-0.5)
    depth = w_qkv.shape[1]
    hidden_width = w_up.shape[2]

    ids = lax.all_gather(jnp.stack([timesteps, labels]), "fsdp", axis=1, tiled=True)
    bias_sizes = [item.shape[1] for item in (b_ada, b_qv, b_out, b_up, b_down)]
    biases = lax.all_gather(
        jnp.concatenate([b_ada[0], b_qv[0], b_out[0], b_up[0], b_down[0]]), "fsdp", axis=0
    )
    bias_full = []
    start = 0
    for size in bias_sizes:
        bias_full.append(biases[:, start : start + size].reshape(-1).astype(jnp.float32))
        start += size
    ada_bias, joined_bias, out_bias, up_bias, down_bias = bias_full

    by_group = w_qkv[0].reshape(depth, 3, groups, band).transpose(2, 0, 1, 3)
    joined_weight = lax.all_gather(
        by_group.reshape(groups, depth, 3 * band), "fsdp", axis=1, tiled=True
    )
    out_weight = lax.all_gather(w_out[0], "fsdp", axis=0, tiled=True).reshape(groups, band, width)
    up_weight = lax.all_gather(w_up[0], "fsdp", axis=0, tiled=True)
    down_weight = lax.all_gather(w_down[0], "fsdp", axis=0, tiled=True)
    bias_qkv = jnp.stack(
        [joined_bias[:width], jnp.zeros((width,), jnp.float32), joined_bias[width:]]
    )
    bias_qkv = bias_qkv.reshape(3, groups, band).transpose(1, 0, 2).reshape(groups, 1, 3 * band)

    time_hot = (ids[0][:, None] == jnp.arange(time_table.shape[0])[None, :]).astype(jnp.bfloat16)
    label_hot = (ids[1][:, None] == jnp.arange(label_table.shape[0])[None, :]).astype(jnp.bfloat16)
    cond = matmul(time_hot, time_table) + matmul(label_hot, label_table)
    scaled = jax.nn.silu(cond).astype(jnp.bfloat16)
    ada_terms = matmul(scaled, w_ada[0]).reshape(shards, lats, 6 * width)
    modulation = jnp.sum(lax.all_to_all(ada_terms, "fsdp", 0, 0), axis=0) + ada_bias
    shift1, scale1, gate1, shift2, scale2, gate2 = (
        part[:, None] for part in jnp.split(modulation, 6, axis=-1)
    )

    def to_heads(item):
        traded = lax.all_to_all(item, "seq", 0, 0)
        span = traded.shape[-1]
        traded = traded.reshape(groups, lats, seq_dev, span).transpose(1, 0, 2, 3)
        return traded.reshape(lats, full_seq, span)

    def to_tokens(item):
        span = item.shape[-1]
        item = item.reshape(lats, groups, seq_dev, span).transpose(1, 0, 2, 3)
        return lax.all_to_all(item.reshape(groups, rows, span), "seq", 0, 0)

    def flat(item):
        return item.reshape(rows, item.shape[-1])

    def tall(item):
        return item.reshape(lats, seq_dev, item.shape[-1])

    def section_forward(field):
        normed, inverse = norm_parts(field)
        first_in = (normed * (1.0 + scale1) + shift1).astype(jnp.bfloat16)
        joined = (dots("rd,pde->pre", flat(first_in), joined_weight) + bias_qkv).astype(
            jnp.bfloat16
        )
        joined = to_heads(joined)
        parts = tuple(by_head(part, heads) for part in jnp.split(joined, 3, axis=-1))
        attended, probs = attend_forward(*parts, factor)
        back = to_tokens(attended.reshape(lats, full_seq, band))
        branch = tall(dots("pre,pef->rf", back, out_weight) + out_bias)
        middle = field + gate1 * branch
        normed_mid, inverse_mid = norm_parts(middle)
        second_in = (normed_mid * (1.0 + scale2) + shift2).astype(jnp.bfloat16)
        hidden = matmul(flat(second_in), up_weight) + up_bias
        active = smooth_gate(hidden).astype(jnp.bfloat16)
        result = tall(matmul(active, down_weight) + down_bias)
        output = (middle + gate2 * result).astype(jnp.bfloat16)
        kept = (
            (normed, inverse, first_in),
            parts + (probs,),
            back,
            branch,
            (normed_mid, inverse_mid, second_in),
            hidden,
            active,
            result,
        )
        return (output, kept)

    def over_shards(part):
        return lax.psum_scatter(part, "fsdp", scatter_dimension=0, tiled=True)

    def held_first(left, right, wanted):
        if not wanted:
            return (right, None)
        term = inner_rows(left, right).astype(jnp.bfloat16)
        return lax.optimization_barrier((right, term))

    def section_backward(upstream, kept, wanted):
        first, attention, back, branch, second, hidden, active, result = kept
        normed, inverse, first_in = first
        normed_mid, inverse_mid, second_in = second
        d_result = (gate2 * upstream).astype(jnp.bfloat16)
        d_result, down_term = held_first(active, flat(d_result), wanted)
        d_active = against(d_result, down_weight)
        _, gate_pull = jax.vjp(smooth_gate, hidden)
        d_hidden = gate_pull(d_active)[0].astype(jnp.bfloat16)
        d_hidden, up_term = held_first(flat(second_in), d_hidden, wanted)
        d_second = tall(against(d_hidden, up_weight))
        d_middle = upstream + norm_back(normed_mid, inverse_mid, d_second * (1.0 + scale2))
        d_branch = flat((gate1 * d_middle).astype(jnp.bfloat16))
        d_back = dots("rf,pef->pre", d_branch, out_weight).astype(jnp.bfloat16)
        d_parts = attend_backward(*attention, by_head(to_heads(d_back), heads), factor)
        d_joined = to_tokens(
            jnp.concatenate([part.reshape(lats, full_seq, band) for part in d_parts], axis=-1)
        )
        if wanted:
            d_joined, down_term = lax.optimization_barrier((d_joined, over_shards(down_term)))
        d_first = tall(dots("pre,pde->rd", d_joined, joined_weight))
        d_field = d_middle + norm_back(normed, inverse, d_first * (1.0 + scale1))
        d_field = d_field.astype(jnp.bfloat16)
        sums = (d_first, d_first * normed, d_middle * branch, d_second, d_second * normed_mid)
        d_mods = jnp.concatenate(
            [jnp.sum(item, axis=1) for item in sums + (upstream * result,)], axis=-1
        )
        return (d_field, d_mods, (d_joined, d_branch, d_hidden, d_result), (down_term, up_term))

    handed, _ = section_forward(section_input.astype(jnp.float32))
    handed = passed_along(handed, "pipe", 1)
    entering = jnp.where(section == 0, section_input, handed)
    section_out, kept = section_forward(entering.astype(jnp.float32))
    handed = section_backward(out_grad.astype(jnp.float32), kept, False)[0]
    handed = passed_along(handed, "pipe", -1)
    upstream = jnp.where(section == 1, out_grad, handed).astype(jnp.float32)
    section_in_grad, d_mods, d_parts, terms = section_backward(upstream, kept, True)
    d_joined, d_branch, d_hidden, d_result = d_parts

    in_order = d_joined.reshape(groups, rows, 3, band).transpose(1, 2, 0, 3)
    in_order = in_order.reshape(rows, 3 * width)
    grad_down = terms[0]
    grad_up = over_shards(terms[1])
    grad_joined = over_shards(inner_rows(flat(kept[0][2]), in_order).astype(jnp.bfloat16))
    out_term = dots("pre,rf->pef", kept[2], d_branch).reshape(width, width)
    grad_out = over_shards(out_term.astype(jnp.bfloat16))
    def over_tokens(part):
        cut_up = part.reshape((groups, part.shape[0] // groups) + part.shape[1:])
        terms = lax.all_to_all(cut_up, "seq", 0, 0).astype(jnp.float32)
        own = jnp.sum(terms, axis=0).astype(jnp.bfloat16)
        whole = lax.all_to_all(jnp.broadcast_to(own[None], cut_up.shape), "seq", 0, 0)
        return whole.reshape(part.shape).astype(jnp.float32)

    grad_down = over_tokens(grad_down)
    grad_up = over_tokens(grad_up)
    grad_joined = over_tokens(grad_joined)
    grad_out = over_tokens(grad_out)

    joined_sums = jnp.sum(d_joined, axis=1, dtype=jnp.float32).reshape(groups, 3, band)
    qv_sums = jnp.stack([joined_sums[:, 0], joined_sums[:, 2]])
    column_sums = [
        qv_sums.reshape(-1),
        jnp.sum(d_branch, axis=0, dtype=jnp.float32),
        jnp.sum(d_hidden, axis=0, dtype=jnp.float32),
        jnp.sum(d_result, axis=0, dtype=jnp.float32),
    ]
    small = jnp.concatenate([d_mods.reshape(-1)] + column_sums)
    small = lax.all_to_all(jnp.broadcast_to(small, (groups, small.size)), "seq", 0, 0)
    small = jnp.sum(small, axis=0)
    mods_sum = jnp.broadcast_to(small[: d_mods.size], (shards, d_mods.size))
    to_shards = [mods_sum]
    cut = d_mods.size
    for part in column_sums:
        to_shards.append(small[cut : cut + part.size].reshape(shards, part.size // shards))
        cut += part.size
    small = lax.all_to_all(jnp.concatenate(to_shards, axis=1), "fsdp", 0, 0)
    d_modulation = small[:, : d_mods.size].reshape(shards * lats, 6 * width).astype(jnp.bfloat16)
    bias_grads = []
    cut = d_mods.size
    for part in to_shards[1:]:
        bias_grads.append(jnp.sum(small[:, cut : cut + part.shape[1]], axis=0)[None])
        cut += part.shape[1]
    ada_sums = jnp.sum(d_modulation, axis=0, dtype=jnp.float32)
    ada_size = 6 * width // shards
    grad_ada_bias = lax.dynamic_slice_in_dim(ada_sums, shard * ada_size, ada_size, 0)[None]
    grad_ada = inner_rows(scaled, d_modulation)
    d_scaled = against(d_modulation, w_ada[0])
    other = lax.ppermute(d_scaled, "pipe", [(0, 1), (1, 0)])
    _, silu_pull = jax.vjp(jax.nn.silu, cond)
    d_cond = silu_pull(d_scaled + other)[0]

    def table_grad(hot):
        return lax.dot_general(
            hot.astype(jnp.float32),
            d_cond,
            (((0,), (0,)), ((), ())),
            precision=lax.Precision.HIGHEST,
        )

    return (
        section_out[None],
        section_in_grad[None],
        table_grad(time_hot),
        table_grad(label_hot),
        grad_ada[None],
        grad_ada_bias,
        grad_joined[None],
        bias_grads[0],
        grad_out[None],
        bias_grads[1],
        grad_up[None],
        bias_grads[2],
        grad_down[None],
        bias_grads[3],
    )


def solution(mesh):
    in_specs = (
        P("fsdp", "seq", None),
        P("fsdp"),
        P("fsdp"),
        P(None, "fsdp"),
        P(None, "fsdp"),
        P("pipe", "fsdp", None),
        P("pipe", "fsdp"),
        P("pipe", "fsdp", None),
        P("pipe", "fsdp"),
        P("pipe", "fsdp", None),
        P("pipe", "fsdp"),
        P("pipe", "fsdp", None),
        P("pipe", "fsdp"),
        P("pipe", "fsdp", None),
        P("pipe", "fsdp"),
        P("fsdp", "seq", None),
    )
    out_specs = (
        P("pipe", "fsdp", "seq", None),
        P("pipe", "fsdp", "seq", None),
        P(None, "fsdp"),
        P(None, "fsdp"),
        P("pipe", "fsdp", None),
        P("pipe", "fsdp"),
        P("pipe", "fsdp", None),
        P("pipe", "fsdp"),
        P("pipe", "fsdp", None),
        P("pipe", "fsdp"),
        P("pipe", "fsdp", None),
        P("pipe", "fsdp"),
        P("pipe", "fsdp", None),
        P("pipe", "fsdp"),
    )
    return jax.shard_map(local, mesh=mesh, in_specs=in_specs, out_specs=out_specs, check_vma=False)
```
